512 devices in a mesh: lat: 16 (over x, z_hi, core), lon: 32 (over y, z_lo).
Axes of the slice: x: 4, y: 4, z: 16 (z_hi: 2, z_lo: 8; z = z_hi * 8 + z_lo), core: 2. Of those that a mesh axis runs over, the one named last changes fastest.
Arguments:
- field: float32 [2, 192, 384, 384], P(None, 'lat', 'lon'), may hold values from -6 to 6
- norm_gain: float32 [2, 384], replicated, may hold values from 0.5 to 1.5
- norm_bias: float32 [2, 384], replicated, may hold values from -3 to 3
- qkv_weight: bfloat16 [2, 384, 1152], replicated, may hold values from -3.7 to 3.7
- qkv_bias: float32 [2, 1152], replicated, may hold values from -2 to 2
- proj_weight: bfloat16 [2, 384, 384], replicated, may hold values from -0.3125 to 0.3125
- proj_bias: float32 [2, 384], replicated, may hold values from -2 to 2
- earth_bias: bfloat16 [2, 16, 12, 6336], P(None, 'lat'), may hold values from -4 to 4
Outputs:
- mixed: float32 [2, 192, 384, 384], P(None, 'lat', 'lon')
The draws below stay inside these ranges and needn't reach their ends.
All inputs are finite; a program needn't handle non-finite values.
Results may differ from the reference program's by a relative error of at most 0.012.
The reference program's roundings to bfloat16 on the way (of `normed`, `packed`, `weights` and `attended`) count: a program that leaves them out, or rounds other values in their place, can miss the bound.
Values may be sent and summed in bfloat16 or wider, within the bound.
No kernel may reach another device: no remote copies, remote signals or barrier semaphores. Data moves between devices by JAX's collectives and lax.ppermute only.
A program may use at most 128 MiB of HBM per device.

```python
import jax
import jax.numpy as jnp
import numpy as np
from jax import lax

C = 384
HEADS = 12
Z = 2
WH = 12
WW = 6
NLAT = 192
NLON = 384
NLW = 16
BIAS_LEN = 6336


def draw_qkv_weight(key, part):
    key = jax.random.fold_in(key, 11)
    base = jnp.clip(jax.random.normal(key, (2, C, 3 * C), jnp.float32), -4.0, 4.0) * C ** (-0.5)
    return base.astype(jnp.bfloat16)


def block_levels(own_key, dims, cuts, least, top_value):
    level = 1.0
    for position, parts in cuts:
        steps = jax.random.uniform(jax.random.fold_in(jax.random.fold_in(own_key, 6), position), (parts,), jnp.float32, least / len(cuts), top_value / len(cuts))
        level = level * jnp.repeat(jnp.exp(steps), dims[position] // parts).reshape((-1,) + (1,) * (len(dims) - 1 - position))
    return level


def bell_draw(key, shape, deviation, limit, cuts=(), dtype=jnp.bfloat16):
    drawn = deviation * jax.random.normal(key, shape, jnp.float32)
    if cuts:
        drawn = drawn * block_levels(key, shape, cuts, -0.22, 0.18)
    return jnp.clip(drawn, -limit, limit).astype(dtype)


def setup_inputs(seed: int = 0) -> dict:
    key_of = jax.random.split(jax.random.key(seed), 9)
    return {
        "field": bell_draw(key_of[0], (Z, NLAT, NLON, C), 1.0, 6.0, ((1, 16), (2, 32)), jnp.float32),
        "norm_gain": jnp.clip(1.0 + 0.1 * jax.random.normal(key_of[1], (2, C), jnp.float32), 0.5, 1.5),
        "norm_bias": bell_draw(key_of[2], (2, C), 0.5, 3.0, (), jnp.float32),
        "qkv_weight": draw_qkv_weight(jax.random.fold_in(key_of[8], 71), 0),
        "qkv_bias": bell_draw(key_of[4], (2, 3 * C), 0.3, 2.0, (), jnp.float32),
        "proj_weight": bell_draw(key_of[5], (2, C, C), C ** -0.5, 0.3125),
        "proj_bias": bell_draw(key_of[6], (2, C), 0.3, 2.0, (), jnp.float32),
        "earth_bias": bell_draw(key_of[7], (2, NLW, HEADS, BIAS_LEN), 1.0, 4.0, ((1, 16),)),
    }


def bias_index(depth, rows, cols):
    level, row, col = np.meshgrid(np.arange(depth), np.arange(rows), np.arange(cols), indexing='ij')
    level = level.reshape(-1)
    row = row.reshape(-1)
    col = col.reshape(-1)
    index = ((level[:, None] * depth + level[None, :]) * rows * rows + row[:, None] * rows + row[None, :]) * (2 * cols - 1)
    index = index + col[:, None] - col[None, :] + cols - 1
    return index.astype(np.int32)

def region_mask(depth, rows, cols):
    level, row, col = np.meshgrid(np.arange(depth), np.arange(rows), np.arange(cols), indexing='ij')
    upper = row.reshape(-1) >= rows - rows // 2
    return np.where(upper[:, None] != upper[None, :], -1000000000.0, 0.0).astype(np.float32)

def layer_norm(grid, gain, offset):
    center = grid - lax.optimization_barrier(jnp.mean(grid, axis=-1, keepdims=True))
    spread = lax.optimization_barrier(jnp.mean(center * center, axis=-1, keepdims=True))
    return (center * lax.rsqrt(spread + 1e-05) * gain + offset).astype(jnp.bfloat16)

def to_windows(grid, rows, cols):
    depth, total_rows, total_cols, width = grid.shape
    shaped = grid.reshape(depth, total_rows // rows, rows, total_cols // cols, cols, width)
    shaped = jnp.transpose(shaped, (1, 3, 0, 2, 4, 5))
    return shaped.reshape(total_rows // rows, total_cols // cols, depth * rows * cols, width)

def from_windows(windows, depth, rows, cols):
    count_a, count_b, tokens_win, width = windows.shape
    shaped = windows.reshape(count_a, count_b, depth, rows, cols, width)
    shaped = jnp.transpose(shaped, (2, 0, 3, 1, 4, 5))
    return shaped.reshape(depth, count_a * rows, count_b * cols, width)

def attend(windows, tables, flags, qkv_w, qkv_b, proj_w, proj_b):
    count_a, count_b, tokens_win, width = windows.shape
    heads = tables.shape[1]
    head_dim = width // heads
    packed = jnp.dot(windows.reshape(-1, width), qkv_w, preferred_element_type=jnp.float32) + qkv_b
    packed = packed.astype(jnp.bfloat16).reshape(count_a, count_b, tokens_win, 3, heads, head_dim)
    query = packed[:, :, :, 0].astype(jnp.float32)
    keys = packed[:, :, :, 1].astype(jnp.float32)
    values = packed[:, :, :, 2].astype(jnp.float32)
    scores = jnp.einsum('abqhd,abkhd->abhqk', query, keys) * head_dim ** (-0.5)
    dense = jnp.take(tables, jnp.asarray(bias_index(Z, WH, WW)), axis=2).astype(jnp.float32)
    masked = jnp.asarray(region_mask(Z, WH, WW))
    scores = scores + dense[:, None] + flags[:, None, None, None, None] * masked
    top = lax.optimization_barrier(jnp.max(scores, axis=-1, keepdims=True))
    expo = jnp.exp(scores - top)
    weights = (expo / lax.optimization_barrier(jnp.sum(expo, axis=-1, keepdims=True))).astype(jnp.bfloat16)
    attended = jnp.einsum('abhqk,abkhd->abqhd', weights.astype(jnp.float32), values).astype(jnp.bfloat16)
    result = jnp.dot(attended.reshape(-1, width), proj_w, preferred_element_type=jnp.float32) + proj_b
    return result.reshape(count_a, count_b, tokens_win, width)

def block(grid, which, shifted, norm_gain, norm_bias, qkv_weight, qkv_bias, proj_weight, proj_bias, earth_bias):
    rolled = jnp.roll(grid, (-(WH // 2), -(WW // 2)), axis=(1, 2)) if shifted else grid
    normed = layer_norm(rolled, norm_gain[which], norm_bias[which])
    windows = to_windows(normed, WH, WW)
    count_lat = windows.shape[0]
    flags = (jnp.arange(count_lat) == count_lat - 1).astype(jnp.float32) * (1.0 if shifted else 0.0)

    def one_window(item):
        win, table, flag = item
        return attend(win[None], table[None], flag[None], qkv_weight[which], qkv_bias[which], proj_weight[which], proj_bias[which])[0]
    result = lax.map(one_window, (windows, earth_bias[which], flags))
    placed = from_windows(result, Z, WH, WW)
    if shifted:
        placed = jnp.roll(placed, (WH // 2, WW // 2), axis=(1, 2))
    return grid + placed

def reference(field, norm_gain, norm_bias, qkv_weight, qkv_bias, proj_weight, proj_bias, earth_bias):
    first = block(field, 0, False, norm_gain, norm_bias, qkv_weight, qkv_bias, proj_weight, proj_bias, earth_bias)
    return block(first, 1, True, norm_gain, norm_bias, qkv_weight, qkv_bias, proj_weight, proj_bias, earth_bias)
```

```python
import functools

import jax
import jax.numpy as jnp
import numpy as np
from jax import lax
from jax.experimental import pallas as pl
from jax.experimental.pallas import tpu as pltpu
from jax.sharding import PartitionSpec as P

Z = 2
WH = 12
WW = 6
HALF = WH // 2
SPAN = 2 * WW - 1
CELLS = WW * Z * HALF
TOKENS = 2 * CELLS
SIDE = CELLS // 2
GROUP = Z * WH
LANES = 128
PAD = 256
PACKED = 3 * LANES
LINE = WH * SPAN
LOG2E = float(np.log2(np.e))
VMEM_LIMIT = 60 * 1024 * 1024


def grid_of(*sizes):
    return [part.reshape(-1) for part in np.meshgrid(*map(np.arange, sizes), indexing="ij")]


def one_hot(rows, columns, width):
    table = np.zeros((len(rows), width), np.float32)
    keep = columns >= 0
    table[np.arange(len(rows))[keep], columns[keep]] = 1.0
    return table


def packed_lane(level, entry):
    lane = (entry + LANES - 2) % PAD
    tail = 2 * LANES + (lane + 64 * level) % LANES
    return np.where(lane >= LANES, level * LANES + lane - LANES, tail)


def lane_selector():
    half, col, level, row = grid_of(2, WW, Z, HALF)
    row = row + half * HALF
    table = np.zeros((PACKED, WW, PAD), np.float32)
    for w in range(WW):
        entry = row * SPAN + w - col + WW - 1
        table[packed_lane(level, entry), w, np.arange(TOKENS)] = 1.0
    return table.reshape(PACKED, WW * PAD)


def full_rows():
    half, col, level, row = grid_of(2, WW, Z, HALF)
    place = col * GROUP + level * WH + half * HALF + row
    return one_hot(place, place, TOKENS)


def table_rows():
    position = np.concatenate([31 - np.arange(32), 47 - np.arange(16)])
    picks = []
    for block in range(2):
        for key_level in range(Z):
            level, row = grid_of(Z, WH)
            picks.append(2 * position[(level * Z + key_level) * WH + row] + block)
    picks = np.concatenate(picks)
    return one_hot(picks, picks, 96)


def native_to_windows(windows):
    window, half, col, level, row = grid_of(windows, 2, WW, Z, HALF)
    place = ((half * HALF + row) * windows * WW + window * WW + col) * Z + level
    return one_hot(place, place, len(place))


def windows_to_native(windows):
    return native_to_windows(windows).T


def strip_from_native(cols):
    half, col, level, row = grid_of(2, cols + WW, Z, HALF)
    own = col - WW // 2
    place = ((half * HALF + row) * cols + own) * Z + level
    place = np.where((own >= 0) & (own < cols), place, -1)
    return one_hot(place, place, WH * cols * Z)


def strip_from_sides(cols):
    half, col, level, row = grid_of(2, cols + WW, Z, HALF)
    own = col - WW // 2
    inside = np.where(own < 0, own + WW, own - cols)
    place = ((half * WW + inside) * Z + level) * HALF + row
    place = np.where((own >= 0) & (own < cols), -1, place)
    return one_hot(place, place, TOKENS)


def native_from_queries():
    row, col, level = grid_of(HALF, 2 * WW, Z)
    middle = (col >= 3) & (col < 9)
    column = np.where(middle, col - 3, np.where(col < 3, col + 3, col - 9))
    place = ((np.where(middle, 0, 1) * WW + column) * Z + level) * HALF + row
    return one_hot(place, place, TOKENS)


def const(table):
    return jnp.asarray(table, jnp.bfloat16)


def exact(table, rows):
    return jnp.dot(table, rows, preferred_element_type=jnp.float32)


def normalized(grid, gain, offset):
    center = grid - jnp.mean(grid, axis=-1, keepdims=True)
    spread = jnp.mean(center * center, axis=-1, keepdims=True)
    return (center * lax.rsqrt(spread + 1e-05) * gain + offset).astype(jnp.bfloat16)


def pack_lines(near, far):
    lane = lax.broadcasted_iota(jnp.int32, near[:, LANES:].shape, 1)
    other = (lane >= 32) & (lane < 96)
    tail = jnp.where(other, pltpu.roll(far[:, :LANES], 64, 1), near[:, :LANES])
    return jnp.concatenate([near[:, LANES:], far[:, LANES:], tail], axis=1)


def table_kernel(raw_ref, pick_ref, first_ref, second_ref, lines):
    heads = raw_ref.shape[0]
    length = raw_ref.shape[2]
    tiles = -(-length // LANES)
    lines[:, 64:96, LANES:] = jnp.zeros((heads, 32, LANES), jnp.float32)
    for tile in range(tiles):
        size = min(LANES, length - tile * LANES)
        block = raw_ref[:, :, tile * LANES : tile * LANES + size].astype(jnp.float32)
        for line in (tile, tile - 1):
            side = (tile - line) * LANES
            if line < 0:
                continue
            if line < 32:
                place = 31 - line
                lines[:, 2 * place : 2 * place + 2, side : side + size] = block
            if line >= 33:
                place = 47 - (line - 33)
                if place >= 32:
                    lines[:, 2 * place : 2 * place + 2, side : side + size] = block
    for head in range(heads):
        rolled = jnp.concatenate(
            [
                pltpu.roll(lines[head, :64], 0, 1, stride=2, stride_axis=0),
                pltpu.roll(lines[head, 64:], 64, 1, stride=2, stride_axis=0),
            ],
            axis=0,
        ).astype(jnp.bfloat16)
        rows = exact(pick_ref[...], rolled)
        first = pltpu.roll(rows[:48], 2, 1)
        at = slice(head * GROUP, (head + 1) * GROUP)
        first_ref[at] = pack_lines(first[:24], first[24:]).astype(jnp.bfloat16)
        second_ref[at] = pack_lines(rows[48:72], rows[72:]).astype(jnp.bfloat16)


def dense_groups(table, lanes, rows, groups):
    spread = exact(table, lanes)
    for group in range(groups):
        part = spread[group * GROUP : (group + 1) * GROUP]
        stacked = jnp.concatenate(
            [part[:, w * PAD : w * PAD + TOKENS] for w in range(WW)], axis=0
        ).astype(jnp.bfloat16)
        yield group, exact(rows, stacked)


def attend(packed, bias, heads):
    rows, width = packed.shape[0], packed.shape[1] // 3
    head_dim = width // heads
    per_tile = LANES // head_dim
    lane = lax.broadcasted_iota(jnp.int32, (rows, LANES), 1) // head_dim
    ones = jnp.ones((rows, LANES), jnp.bfloat16)
    tiles = []
    for start in range(0, width, LANES):
        query, keys, values = (
            packed[:, start + i * width : start + i * width + LANES] for i in range(3)
        )
        values = jnp.concatenate([values, ones], axis=1)
        total = jnp.zeros((rows, LANES), jnp.float32)
        for part in range(per_tile):
            mine = lane == part
            chosen = jnp.where(mine, query, jnp.zeros_like(query))
            scores = lax.dot_general(
                chosen, keys, (((1,), (1,)), ((), ())), preferred_element_type=jnp.float32
            )
            scores = scores * (LOG2E * head_dim ** (-0.5)) + bias(start // head_dim + part)
            top = jnp.max(scores, axis=-1, keepdims=True)
            weights = jnp.exp2(scores - top).astype(jnp.bfloat16)
            mixed = jnp.dot(weights, values, preferred_element_type=jnp.float32)
            total = jnp.where(mine, mixed[:, :LANES] / mixed[:, LANES:], total)
        tiles.append(total)
    return jnp.concatenate(tiles, axis=1)


def inner_columns(rows, width):
    index = lax.broadcasted_iota(jnp.int32, (rows, width), 0)
    return index - jnp.where(index >= CELLS, CELLS, 0) < SIDE


def first_kernel(
    heads, field_ref, gain_ref, offset_ref, qkv_w, qkv_b, proj_w, proj_b, table_ref, lanes_ref,
    rows_ref, order_ref, back_ref, first_ref, second_ref, bias_ref, core_ref,
):
    for head, dense in dense_groups(table_ref[...], lanes_ref[...], rows_ref[...], heads):
        bias_ref[head] = dense * LOG2E
    cells, depth, width = field_ref.shape
    grid = field_ref[...].reshape(cells * depth, width)
    tokens = normalized(grid, gain_ref[0:1], offset_ref[0:1])
    tokens = exact(order_ref[...], tokens).astype(jnp.bfloat16)
    packed = jnp.dot(tokens, qkv_w[...], preferred_element_type=jnp.float32) + qkv_b[0:1]
    packed = packed.astype(jnp.bfloat16)
    for window in range(2):
        at = slice(window * TOKENS, (window + 1) * TOKENS)
        core_ref[at] = attend(packed[at], bias_ref.__getitem__, heads)
    core = exact(back_ref[...], core_ref[...].astype(jnp.bfloat16)).astype(jnp.bfloat16)
    result = jnp.dot(core, proj_w[...], preferred_element_type=jnp.float32) + proj_b[0:1]
    first = grid + result
    first_ref[...] = first
    second_ref[...] = normalized(first, gain_ref[1:2], offset_ref[1:2])


def edge_kernel(
    heads, place_ref, second_ref, near_ref, wrap_ref, gain_ref, offset_ref, qkv_w, qkv_b, proj_w,
    proj_b, bias_ref, side_ref, strip_ref, edge_ref, send_ref, keep_ref, core_ref,
):
    width = second_ref.shape[1]
    near = near_ref[...].astype(jnp.float32).reshape(TOKENS, width)
    wrap = wrap_ref[...].astype(jnp.float32).reshape(TOKENS, width)
    odd = place_ref[1] == 1
    left = exact(side_ref[...], jnp.where(odd, near, wrap).astype(jnp.bfloat16))
    right = exact(side_ref[...], jnp.where(odd, wrap, near).astype(jnp.bfloat16))
    tokens = normalized(jnp.concatenate([left, right], axis=0), gain_ref[0:1], offset_ref[0:1])
    packed = jnp.dot(tokens, qkv_w[...], preferred_element_type=jnp.float32) + qkv_b[0:1]
    packed = packed.astype(jnp.bfloat16)
    for window in range(2):
        at = slice(window * TOKENS, (window + 1) * TOKENS)
        core_ref[at] = attend(packed[at], bias_ref.__getitem__, heads)
    inner = inner_columns(TOKENS, width)
    core = jnp.where(inner, core_ref[TOKENS:], core_ref[:TOKENS]).astype(jnp.bfloat16)
    result = jnp.dot(core, proj_w[...], preferred_element_type=jnp.float32) + proj_b[0:1]
    edge = jnp.where(inner, right, left) + result
    edge = normalized(edge, gain_ref[1:2], offset_ref[1:2])
    strip = exact(strip_ref[...], second_ref[...]) + exact(edge_ref[...], edge)
    half = strip.shape[0] // 2
    send_ref[...] = strip[:half].astype(jnp.bfloat16)
    keep_ref[...] = strip[half:].astype(jnp.bfloat16)


def bias_kernel(heads, flag_ref, table_ref, lanes_ref, rows_ref, out_ref):
    upper = lax.broadcasted_iota(jnp.int32, (TOKENS, TOKENS), 0) < CELLS
    left = lax.broadcasted_iota(jnp.int32, (TOKENS, TOKENS), 1) < CELLS
    barred = jnp.where(upper != left, flag_ref[0] * -1000000000.0, 0.0)
    for head, dense in dense_groups(table_ref[...], lanes_ref[...], rows_ref[...], heads):
        out_ref[head] = (dense + barred) * LOG2E


def second_kernel(
    heads, own_ref, got_ref, qkv_w, qkv_b, proj_w, proj_b, bias_ref, back_ref, keep_ref, send_ref,
    core_ref,
):
    width = own_ref.shape[1]
    own, got = own_ref[...].astype(jnp.float32), got_ref[...].astype(jnp.float32)
    tokens = []
    for window in range(3):
        at = slice(window * CELLS, (window + 1) * CELLS)
        tokens += [own[at], got[at]]
    tokens = jnp.concatenate(tokens, axis=0).astype(jnp.bfloat16)
    packed = jnp.dot(tokens, qkv_w[...], preferred_element_type=jnp.float32) + qkv_b[1:2]
    packed = packed.astype(jnp.bfloat16)
    for window in range(3):
        at = slice(window * TOKENS, (window + 1) * TOKENS)
        core_ref[window] = attend(packed[at], bias_ref.__getitem__, heads)
    inner = inner_columns(CELLS, width)
    for start, out_ref in ((CELLS, send_ref), (0, keep_ref)):
        at = slice(start, start + CELLS)
        outer = jnp.where(inner, core_ref[2, at], core_ref[0, at])
        core = jnp.concatenate([core_ref[1, at], outer], axis=0).astype(jnp.bfloat16)
        core = exact(back_ref[...], core).astype(jnp.bfloat16)
        result = jnp.dot(core, proj_w[...], preferred_element_type=jnp.float32) + proj_b[1:2]
        out_ref[...] = result.astype(out_ref.dtype)


def final_kernel(first_ref, keep_ref, got_ref, out_ref):
    got = got_ref[...].astype(jnp.float32)
    result = first_ref[...] + jnp.concatenate([got, keep_ref[...]], axis=0)
    out_ref[...] = result.reshape(out_ref.shape)


def exchanged(block, near):
    count = lax.axis_size("lon")
    partner = [i ^ 1 if near else (i + (1 if i % 2 else -1)) % count for i in range(count)]
    return lax.ppermute(block, "lon", [(i, partner[i]) for i in range(count)])


def passed_along(block, axis, distance):
    count = lax.axis_size(axis)
    return lax.ppermute(block, axis, [((i - distance) % count, i) for i in range(count)])


VMEM = pl.BlockSpec(memory_space=pltpu.VMEM)
SMEM = pl.BlockSpec(memory_space=pltpu.SMEM)
WHOLE = lambda shape: pl.BlockSpec(shape, lambda i: (0,) * len(shape))


def chosen(array, which):
    size = array.shape[1:]
    return pl.BlockSpec((None, *size), lambda i: (which,) + (0,) * len(size))


def run(kernel, name, operands, specs, outs, scratch=(), flops=10**9):
    specs = [WHOLE(x.shape) if s is None else s for x, s in zip(operands, specs, strict=True)]
    return pl.pallas_call(
        kernel,
        grid=(1,),
        out_shape=[jax.ShapeDtypeStruct(*out) for out in outs],
        in_specs=specs,
        out_specs=[WHOLE(shape) for shape, _ in outs],
        scratch_shapes=list(scratch),
        compiler_params=pltpu.CompilerParams(vmem_limit_bytes=VMEM_LIMIT),
        cost_estimate=pl.CostEstimate(flops=flops, bytes_accessed=4000000, transcendentals=0),
        name=name,
    )(*operands)


def per_device(
    field, norm_gain, norm_bias, qkv_weight, qkv_bias, proj_weight, proj_bias, earth_bias
):
    depth, lat_rows, lon_cols, width = field.shape
    heads = earth_bias.shape[2]
    f32, bf16 = jnp.float32, jnp.bfloat16
    lat, lon = lax.axis_index("lat"), lax.axis_index("lon")
    place = jnp.stack([lat % 2, lon % 2]).astype(jnp.int32)
    last = (lat == lax.axis_size("lat") - 1).astype(f32).reshape(1)
    native = jnp.transpose(field, (1, 2, 0, 3))
    raw = jnp.transpose(earth_bias[:, 0], (1, 0, 2))

    halves = native.astype(bf16)
    odd = place[1] == 1
    to_wrap = jnp.where(odd, halves[:, WW:], halves[:, :WW])
    to_near = jnp.where(odd, halves[:, :WW], halves[:, WW:])
    wrap = exchanged(to_wrap, False)
    near = exchanged(to_near, True)

    rows = heads * WH
    lanes = const(lane_selector())
    table0, table1 = run(
        table_kernel,
        "tables",
        (raw, const(table_rows())),
        (None, None),
        [((2 * rows, PACKED), bf16)] * 2,
        [pltpu.VMEM((heads, 96, PAD), f32)],
    )
    strip = (lon_cols + WW) * Z * HALF
    cells = lat_rows * lon_cols
    first, second, bias0 = run(
        functools.partial(first_kernel, heads),
        "first_block",
        (
            native.reshape(cells, depth, width), norm_gain, norm_bias, qkv_weight, qkv_bias,
            proj_weight, proj_bias, table0, lanes, const(full_rows()),
            const(native_to_windows(2)), const(windows_to_native(2)),
        ),
        (None, None, None, chosen(qkv_weight, 0), None, chosen(proj_weight, 0)) + (None,) * 6,
        [((cells * depth, width), f32), ((cells * depth, width), bf16), ((heads, TOKENS, TOKENS), f32)],
        [pltpu.VMEM((2 * TOKENS, width), f32)],
    )
    send, keep = run(
        functools.partial(edge_kernel, heads),
        "first_block_edges",
        (
            place, second, near.reshape(cells // 2, depth, width),
            wrap.reshape(cells // 2, depth, width), norm_gain, norm_bias, qkv_weight, qkv_bias,
            proj_weight, proj_bias, bias0, const(native_to_windows(1)),
            const(strip_from_native(lon_cols)), const(strip_from_sides(lon_cols)),
        ),
        (SMEM, None, None, None, None, None, chosen(qkv_weight, 0), None, chosen(proj_weight, 0))
        + (None,) * 5,
        [((strip, width), bf16), ((strip, width), bf16)],
        [pltpu.VMEM((2 * TOKENS, width), f32)],
    )
    from_above = passed_along(send, "lat", -1)
    (bias1,) = run(
        functools.partial(bias_kernel, heads),
        "second_bias",
        (last, table1, lanes, const(full_rows())),
        (SMEM, None, None, None),
        [((heads, TOKENS, TOKENS), f32)],
    )
    kept, leaving = run(
        functools.partial(second_kernel, heads),
        "second_block",
        (
            keep, from_above, qkv_weight, qkv_bias, proj_weight, proj_bias, bias1,
            const(native_from_queries()),
        ),
        (None, None, chosen(qkv_weight, 1), None, chosen(proj_weight, 1)) + (None,) * 3,
        [((TOKENS, width), f32), ((TOKENS, width), bf16)],
        [pltpu.VMEM((3, TOKENS, width), f32)],
    )
    from_below = passed_along(leaving, "lat", 1)
    (mixed,) = run(
        final_kernel,
        "final_sum",
        (first, kept, from_below),
        (None,) * 3,
        [((cells, depth, width), f32)],
    )
    return jnp.transpose(mixed.reshape(lat_rows, lon_cols, depth, width), (2, 0, 1, 3))


def solution(mesh):
    in_specs = (P(None, "lat", "lon", None), P(), P(), P(), P(), P(), P(), P(None, "lat", None, None))
    out_specs = P(None, "lat", "lon", None)
    return jax.shard_map(
        per_device, mesh=mesh, in_specs=in_specs, out_specs=out_specs, check_vma=False
    )
```

```python
import functools

import jax
import jax.numpy as jnp
import numpy as np
from jax import lax
from jax.experimental import pallas as pl
from jax.experimental.pallas import tpu as pltpu
from jax.sharding import PartitionSpec as P

Z = 2
WH = 12
WW = 6
HALF = WH // 2
SPAN = 2 * WW - 1
CELLS = WW * Z * HALF
TOKENS = 2 * CELLS
SIDE = CELLS // 2
GROUP = Z * WH
LANES = 128
PAD = 256
PACKED = 3 * LANES
LINE = WH * SPAN
LOG2E = float(np.log2(np.e))
VMEM_LIMIT = 60 * 1024 * 1024
VMEM_SHARED = 40 * 1024 * 1024


def grid_of(*sizes):
    return [part.reshape(-1) for part in np.meshgrid(*map(np.arange, sizes), indexing="ij")]


def one_hot(rows, columns, width):
    table = np.zeros((len(rows), width), np.float32)
    keep = columns >= 0
    table[np.arange(len(rows))[keep], columns[keep]] = 1.0
    return table


def packed_lane(level, entry):
    lane = (entry + LANES - 2) % PAD
    tail = 2 * LANES + (lane + 64 * level) % LANES
    return np.where(lane >= LANES, level * LANES + lane - LANES, tail)


def lane_selector():
    half, col, level, row = grid_of(2, WW, Z, HALF)
    row = row + half * HALF
    table = np.zeros((PACKED, WW, PAD), np.float32)
    for w in range(WW):
        entry = row * SPAN + w - col + WW - 1
        table[packed_lane(level, entry), w, np.arange(TOKENS)] = 1.0
    return table.reshape(PACKED, WW * PAD)


def full_rows():
    half, col, level, row = grid_of(2, WW, Z, HALF)
    place = col * GROUP + level * WH + half * HALF + row
    return one_hot(place, place, TOKENS)


def table_rows():
    position = np.concatenate([31 - np.arange(32), 47 - np.arange(16)])
    picks = []
    for block in range(2):
        for key_level in range(Z):
            level, row = grid_of(Z, WH)
            picks.append(2 * position[(level * Z + key_level) * WH + row] + block)
    picks = np.concatenate(picks)
    return one_hot(picks, picks, 96)


def native_to_windows(windows):
    window, half, col, level, row = grid_of(windows, 2, WW, Z, HALF)
    place = ((half * HALF + row) * windows * WW + window * WW + col) * Z + level
    return one_hot(place, place, len(place))


def windows_to_native(windows):
    return native_to_windows(windows).T


def strip_from_native(cols):
    half, col, level, row = grid_of(2, cols + WW, Z, HALF)
    own = col - WW // 2
    place = ((half * HALF + row) * cols + own) * Z + level
    place = np.where((own >= 0) & (own < cols), place, -1)
    return one_hot(place, place, WH * cols * Z)


def strip_from_sides(cols):
    half, col, level, row = grid_of(2, cols + WW, Z, HALF)
    own = col - WW // 2
    inside = np.where(own < 0, own + WW, own - cols)
    place = ((half * WW + inside) * Z + level) * HALF + row
    place = np.where((own >= 0) & (own < cols), -1, place)
    return one_hot(place, place, TOKENS)


def native_from_queries():
    row, col, level = grid_of(HALF, 2 * WW, Z)
    middle = (col >= 3) & (col < 9)
    column = np.where(middle, col - 3, np.where(col < 3, col + 3, col - 9))
    place = ((np.where(middle, 0, 1) * WW + column) * Z + level) * HALF + row
    return one_hot(place, place, TOKENS)


def const(table):
    return jnp.asarray(table, jnp.bfloat16)


def exact(table, rows):
    return jnp.dot(table, rows, preferred_element_type=jnp.float32)


def normalized(grid, gain, offset):
    center = grid - jnp.mean(grid, axis=-1, keepdims=True)
    spread = jnp.mean(center * center, axis=-1, keepdims=True)
    return (center * lax.rsqrt(spread + 1e-05) * gain + offset).astype(jnp.bfloat16)


def pack_lines(near, far):
    lane = lax.broadcasted_iota(jnp.int32, near[:, LANES:].shape, 1)
    other = (lane >= 32) & (lane < 96)
    tail = jnp.where(other, pltpu.roll(far[:, :LANES], 64, 1), near[:, :LANES])
    return jnp.concatenate([near[:, LANES:], far[:, LANES:], tail], axis=1)


def table_kernel(raw_ref, pick_ref, first_ref, second_ref, lines):
    heads = raw_ref.shape[0]
    length = raw_ref.shape[2]
    tiles = -(-length // LANES)
    lines[:, 64:96, LANES:] = jnp.zeros((heads, 32, LANES), jnp.float32)
    for tile in range(tiles):
        size = min(LANES, length - tile * LANES)
        block = raw_ref[:, :, tile * LANES : tile * LANES + size].astype(jnp.float32)
        for line in (tile, tile - 1):
            side = (tile - line) * LANES
            if line < 0:
                continue
            if line < 32:
                place = 31 - line
                lines[:, 2 * place : 2 * place + 2, side : side + size] = block
            if line >= 33:
                place = 47 - (line - 33)
                if place >= 32:
                    lines[:, 2 * place : 2 * place + 2, side : side + size] = block
    for head in range(heads):
        rolled = jnp.concatenate(
            [
                pltpu.roll(lines[head, :64], 0, 1, stride=2, stride_axis=0),
                pltpu.roll(lines[head, 64:], 64, 1, stride=2, stride_axis=0),
            ],
            axis=0,
        ).astype(jnp.bfloat16)
        rows = exact(pick_ref[...], rolled)
        first = pltpu.roll(rows[:48], 2, 1)
        at = slice(head * GROUP, (head + 1) * GROUP)
        first_ref[at] = pack_lines(first[:24], first[24:]).astype(jnp.bfloat16)
        second_ref[at] = pack_lines(rows[48:72], rows[72:]).astype(jnp.bfloat16)


def dense_groups(table, lanes, rows, groups):
    spread = exact(table, lanes)
    for group in range(groups):
        part = spread[group * GROUP : (group + 1) * GROUP]
        stacked = jnp.concatenate(
            [part[:, w * PAD : w * PAD + TOKENS] for w in range(WW)], axis=0
        ).astype(jnp.bfloat16)
        yield group, exact(rows, stacked)


def attend(packed, bias, heads):
    rows, width = packed.shape[0], packed.shape[1] // 3
    head_dim = width // heads
    per_tile = LANES // head_dim
    lane = lax.broadcasted_iota(jnp.int32, (rows, LANES), 1) // head_dim
    ones = jnp.ones((rows, LANES), jnp.bfloat16)
    tiles = []
    for start in range(0, width, LANES):
        query, keys, values = (
            packed[:, start + i * width : start + i * width + LANES] for i in range(3)
        )
        values = jnp.concatenate([values, ones], axis=1)
        total = jnp.zeros((rows, LANES), jnp.float32)
        for part in range(per_tile):
            mine = lane == part
            chosen = jnp.where(mine, query, jnp.zeros_like(query))
            scores = lax.dot_general(
                chosen, keys, (((1,), (1,)), ((), ())), preferred_element_type=jnp.float32
            )
            scores = scores * (LOG2E * head_dim ** (-0.5)) + bias(start // head_dim + part)
            top = jnp.max(scores, axis=-1, keepdims=True)
            weights = jnp.exp2(scores - top).astype(jnp.bfloat16)
            mixed = jnp.dot(weights, values, preferred_element_type=jnp.float32)
            total = jnp.where(mine, mixed[:, :LANES] / mixed[:, LANES:], total)
        tiles.append(total)
    return jnp.concatenate(tiles, axis=1)


def inner_columns(rows, width):
    index = lax.broadcasted_iota(jnp.int32, (rows, width), 0)
    return index - jnp.where(index >= CELLS, CELLS, 0) < SIDE


def first_kernel(
    heads, field_ref, gain_ref, offset_ref, qkv_w, qkv_b, proj_w, proj_b, table_ref, lanes_ref,
    rows_ref, order_ref, back_ref, first_ref, second_ref, bias_ref, core_ref,
):
    for head, dense in dense_groups(table_ref[...], lanes_ref[...], rows_ref[...], heads):
        bias_ref[head] = dense * LOG2E
    cells, depth, width = field_ref.shape
    grid = field_ref[...].reshape(cells * depth, width)
    tokens = normalized(grid, gain_ref[0:1], offset_ref[0:1])
    tokens = exact(order_ref[...], tokens).astype(jnp.bfloat16)
    packed = jnp.dot(tokens, qkv_w[...], preferred_element_type=jnp.float32) + qkv_b[0:1]
    packed = packed.astype(jnp.bfloat16)
    for window in range(2):
        at = slice(window * TOKENS, (window + 1) * TOKENS)
        core_ref[at] = attend(packed[at], bias_ref.__getitem__, heads)
    core = exact(back_ref[...], core_ref[...].astype(jnp.bfloat16)).astype(jnp.bfloat16)
    result = jnp.dot(core, proj_w[...], preferred_element_type=jnp.float32) + proj_b[0:1]
    first = grid + result
    first_ref[...] = first
    second_ref[...] = normalized(first, gain_ref[1:2], offset_ref[1:2])


def edge_kernel(
    heads, second_ref, near_ref, wrap_ref, gain_ref, offset_ref, qkv_w, qkv_b, proj_w,
    proj_b, bias_ref, side_ref, strip_ref, edge_ref, send_ref, keep_ref, core_ref,
):
    width = second_ref.shape[1]
    near = near_ref[...].astype(jnp.float32).reshape(TOKENS, width)
    wrap = wrap_ref[...].astype(jnp.float32).reshape(TOKENS, width)
    odd = lax.rem(lax.axis_index("lon"), 2) == 1
    left = exact(side_ref[...], jnp.where(odd, near, wrap).astype(jnp.bfloat16))
    right = exact(side_ref[...], jnp.where(odd, wrap, near).astype(jnp.bfloat16))
    tokens = normalized(jnp.concatenate([left, right], axis=0), gain_ref[0:1], offset_ref[0:1])
    packed = jnp.dot(tokens, qkv_w[...], preferred_element_type=jnp.float32) + qkv_b[0:1]
    packed = packed.astype(jnp.bfloat16)
    for window in range(2):
        at = slice(window * TOKENS, (window + 1) * TOKENS)
        core_ref[at] = attend(packed[at], bias_ref.__getitem__, heads)
    inner = inner_columns(TOKENS, width)
    core = jnp.where(inner, core_ref[TOKENS:], core_ref[:TOKENS]).astype(jnp.bfloat16)
    result = jnp.dot(core, proj_w[...], preferred_element_type=jnp.float32) + proj_b[0:1]
    edge = jnp.where(inner, right, left) + result
    edge = normalized(edge, gain_ref[1:2], offset_ref[1:2])
    strip = exact(strip_ref[...], second_ref[...]) + exact(edge_ref[...], edge)
    half = strip.shape[0] // 2
    send_ref[...] = strip[:half].astype(jnp.bfloat16)
    keep_ref[...] = strip[half:].astype(jnp.bfloat16)


def bias_kernel(heads, table_ref, lanes_ref, rows_ref, out_ref):
    upper = lax.broadcasted_iota(jnp.int32, (TOKENS, TOKENS), 0) < CELLS
    left = lax.broadcasted_iota(jnp.int32, (TOKENS, TOKENS), 1) < CELLS
    last = lax.axis_index("lat") == lax.axis_size("lat") - 1
    flag = jnp.where(last, 1.0, 0.0)
    barred = jnp.where(upper != left, flag * -1000000000.0, 0.0)
    for head, dense in dense_groups(table_ref[...], lanes_ref[...], rows_ref[...], heads):
        out_ref[head] = (dense + barred) * LOG2E


def second_kernel(
    heads, own_ref, got_ref, qkv_w, qkv_b, proj_w, proj_b, bias_ref, back_ref, keep_ref, send_ref,
    core_ref,
):
    width = own_ref.shape[1]
    own, got = own_ref[...].astype(jnp.float32), got_ref[...].astype(jnp.float32)
    tokens = []
    for window in range(3):
        at = slice(window * CELLS, (window + 1) * CELLS)
        tokens += [own[at], got[at]]
    tokens = jnp.concatenate(tokens, axis=0).astype(jnp.bfloat16)
    packed = jnp.dot(tokens, qkv_w[...], preferred_element_type=jnp.float32) + qkv_b[1:2]
    packed = packed.astype(jnp.bfloat16)
    for window in range(3):
        at = slice(window * TOKENS, (window + 1) * TOKENS)
        core_ref[window] = attend(packed[at], bias_ref.__getitem__, heads)
    inner = inner_columns(CELLS, width)
    for start, out_ref in ((CELLS, send_ref), (0, keep_ref)):
        at = slice(start, start + CELLS)
        outer = jnp.where(inner, core_ref[2, at], core_ref[0, at])
        core = jnp.concatenate([core_ref[1, at], outer], axis=0).astype(jnp.bfloat16)
        core = exact(back_ref[...], core).astype(jnp.bfloat16)
        result = jnp.dot(core, proj_w[...], preferred_element_type=jnp.float32) + proj_b[1:2]
        out_ref[...] = result.astype(out_ref.dtype)


def final_kernel(first_ref, keep_ref, got_ref, out_ref):
    got = got_ref[...].astype(jnp.float32)
    result = first_ref[...] + jnp.concatenate([got, keep_ref[...]], axis=0)
    out_ref[...] = result.reshape(out_ref.shape)


def exchanged(block, near):
    count = lax.axis_size("lon")
    partner = [i ^ 1 if near else (i + (1 if i % 2 else -1)) % count for i in range(count)]
    return lax.ppermute(block, "lon", [(i, partner[i]) for i in range(count)])


def passed_along(block, axis, distance):
    count = lax.axis_size(axis)
    return lax.ppermute(block, axis, [((i - distance) % count, i) for i in range(count)])


WHOLE = lambda shape: pl.BlockSpec(shape, lambda i: (0,) * len(shape))


def chosen(array, which):
    size = array.shape[1:]
    return pl.BlockSpec((None, *size), lambda i: (which,) + (0,) * len(size))


def run(kernel, name, operands, specs, outs, scratch=(), limit=VMEM_LIMIT):
    specs = [WHOLE(x.shape) if s is None else s for x, s in zip(operands, specs, strict=True)]
    return pl.pallas_call(
        kernel,
        grid=(1,),
        out_shape=[jax.ShapeDtypeStruct(*out) for out in outs],
        in_specs=specs,
        out_specs=[WHOLE(shape) for shape, _ in outs],
        scratch_shapes=list(scratch),
        compiler_params=pltpu.CompilerParams(vmem_limit_bytes=limit),
        cost_estimate=pl.CostEstimate(flops=10**9, bytes_accessed=4000000, transcendentals=0),
        name=name,
    )(*operands)


def per_device(
    field, norm_gain, norm_bias, qkv_weight, qkv_bias, proj_weight, proj_bias, earth_bias
):
    depth, lat_rows, lon_cols, width = field.shape
    heads = earth_bias.shape[2]
    f32, bf16 = jnp.float32, jnp.bfloat16
    native = jnp.transpose(field, (1, 2, 0, 3))
    raw = jnp.transpose(earth_bias[:, 0], (1, 0, 2))

    halves = native.astype(bf16)
    odd = lax.axis_index("lon") % 2 == 1
    to_wrap = jnp.where(odd, halves[:, WW:], halves[:, :WW])
    to_near = jnp.where(odd, halves[:, :WW], halves[:, WW:])
    wrap = exchanged(to_wrap, False)
    near = exchanged(to_near, True)

    rows = heads * WH
    lanes = const(lane_selector())
    table0, table1 = run(
        table_kernel,
        "tables",
        (raw, const(table_rows())),
        (None, None),
        [((2 * rows, PACKED), bf16)] * 2,
        [pltpu.VMEM((heads, 96, PAD), f32)],
    )
    strip = (lon_cols + WW) * Z * HALF
    cells = lat_rows * lon_cols
    first, second, bias0 = run(
        functools.partial(first_kernel, heads),
        "first_block",
        (
            native.reshape(cells, depth, width), norm_gain, norm_bias, qkv_weight, qkv_bias,
            proj_weight, proj_bias, table0, lanes, const(full_rows()),
            const(native_to_windows(2)), const(windows_to_native(2)),
        ),
        (None, None, None, chosen(qkv_weight, 0), None, chosen(proj_weight, 0)) + (None,) * 6,
        [((cells * depth, width), f32), ((cells * depth, width), bf16), ((heads, TOKENS, TOKENS), f32)],
        [pltpu.VMEM((2 * TOKENS, width), f32)],
    )
    send, keep = run(
        functools.partial(edge_kernel, heads),
        "first_block_edges",
        (
            second, near.reshape(cells // 2, depth, width),
            wrap.reshape(cells // 2, depth, width), norm_gain, norm_bias, qkv_weight, qkv_bias,
            proj_weight, proj_bias, bias0, const(native_to_windows(1)),
            const(strip_from_native(lon_cols)), const(strip_from_sides(lon_cols)),
        ),
        (None, None, None, None, None, chosen(qkv_weight, 0), None, chosen(proj_weight, 0))
        + (None,) * 5,
        [((strip, width), bf16), ((strip, width), bf16)],
        [pltpu.VMEM((2 * TOKENS, width), f32)],
        limit=VMEM_SHARED,
    )
    from_above = passed_along(send, "lat", -1)
    (bias1,) = run(
        functools.partial(bias_kernel, heads),
        "second_bias",
        (table1, lanes, const(full_rows())),
        (None, None, None),
        [((heads, TOKENS, TOKENS), f32)],
        limit=VMEM_SHARED,
    )
    kept, leaving = run(
        functools.partial(second_kernel, heads),
        "second_block",
        (
            keep, from_above, qkv_weight, qkv_bias, proj_weight, proj_bias, bias1,
            const(native_from_queries()),
        ),
        (None, None, chosen(qkv_weight, 1), None, chosen(proj_weight, 1)) + (None,) * 3,
        [((TOKENS, width), f32), ((TOKENS, width), bf16)],
        [pltpu.VMEM((3, TOKENS, width), f32)],
        limit=VMEM_SHARED,
    )
    from_below = passed_along(leaving, "lat", 1)
    (mixed,) = run(
        final_kernel,
        "final_sum",
        (first, kept, from_below),
        (None,) * 3,
        [((cells, depth, width), f32)],
        limit=VMEM_SHARED,
    )
    return jnp.transpose(mixed.reshape(lat_rows, lon_cols, depth, width), (2, 0, 1, 3))


def solution(mesh):
    in_specs = (P(None, "lat", "lon", None), P(), P(), P(), P(), P(), P(), P(None, "lat", None, None))
    out_specs = P(None, "lat", "lon", None)
    return jax.shard_map(
        per_device, mesh=mesh, in_specs=in_specs, out_specs=out_specs, check_vma=False
    )
```

```python
import functools

import jax
import jax.numpy as jnp
import numpy as np
from jax import lax
from jax.experimental import pallas as pl
from jax.experimental.pallas import tpu as pltpu
from jax.sharding import PartitionSpec as P

Z = 2
WH = 12
WW = 6
HALF = WH // 2
SPAN = 2 * WW - 1
CELLS = WW * Z * HALF
TOKENS = 2 * CELLS
SIDE = CELLS // 2
GROUP = Z * WH
LANES = 128
PAD = 256
PACKED = 3 * LANES
LINE = WH * SPAN
LOG2E = float(np.log2(np.e))
VMEM_LIMIT = 60 * 1024 * 1024
VMEM_SHARED = 40 * 1024 * 1024


def grid_of(*sizes):
    return [part.reshape(-1) for part in np.meshgrid(*map(np.arange, sizes), indexing="ij")]


def one_hot(rows, columns, width):
    table = np.zeros((len(rows), width), np.float32)
    keep = columns >= 0
    table[np.arange(len(rows))[keep], columns[keep]] = 1.0
    return table


def packed_lane(level, entry):
    lane = (entry + LANES - 2) % PAD
    tail = 2 * LANES + (lane + 64 * level) % LANES
    return np.where(lane >= LANES, level * LANES + lane - LANES, tail)


def lane_selector():
    half, col, level, row = grid_of(2, WW, Z, HALF)
    row = row + half * HALF
    table = np.zeros((PACKED, WW, PAD), np.float32)
    for w in range(WW):
        entry = row * SPAN + w - col + WW - 1
        table[packed_lane(level, entry), w, np.arange(TOKENS)] = 1.0
    return table.reshape(PACKED, WW * PAD)


def full_rows():
    half, col, level, row = grid_of(2, WW, Z, HALF)
    place = col * GROUP + level * WH + half * HALF + row
    return one_hot(place, place, TOKENS)


def table_rows():
    position = np.concatenate([31 - np.arange(32), 47 - np.arange(16)])
    picks = []
    for block in range(2):
        for key_level in range(Z):
            level, row = grid_of(Z, WH)
            picks.append(2 * position[(level * Z + key_level) * WH + row] + block)
    picks = np.concatenate(picks)
    return one_hot(picks, picks, 96)


def native_to_windows(windows):
    window, half, col, level, row = grid_of(windows, 2, WW, Z, HALF)
    place = ((half * HALF + row) * windows * WW + window * WW + col) * Z + level
    return one_hot(place, place, len(place))


def windows_to_native(windows):
    return native_to_windows(windows).T


def strip_from_native(cols):
    half, col, level, row = grid_of(2, cols + WW, Z, HALF)
    own = col - WW // 2
    place = ((half * HALF + row) * cols + own) * Z + level
    place = np.where((own >= 0) & (own < cols), place, -1)
    return one_hot(place, place, WH * cols * Z)


def strip_from_sides(cols):
    half, col, level, row = grid_of(2, cols + WW, Z, HALF)
    own = col - WW // 2
    inside = np.where(own < 0, own + WW, own - cols)
    place = ((half * WW + inside) * Z + level) * HALF + row
    place = np.where((own >= 0) & (own < cols), -1, place)
    return one_hot(place, place, TOKENS)


def native_from_queries():
    row, col, level = grid_of(HALF, 2 * WW, Z)
    middle = (col >= 3) & (col < 9)
    column = np.where(middle, col - 3, np.where(col < 3, col + 3, col - 9))
    place = ((np.where(middle, 0, 1) * WW + column) * Z + level) * HALF + row
    return one_hot(place, place, TOKENS)


def const(table):
    return jnp.asarray(table, jnp.bfloat16)


def exact(table, rows):
    return jnp.dot(table, rows, preferred_element_type=jnp.float32)


def normalized(grid, gain, offset):
    center = grid - jnp.mean(grid, axis=-1, keepdims=True)
    spread = jnp.mean(center * center, axis=-1, keepdims=True)
    return (center * lax.rsqrt(spread + 1e-05) * gain + offset).astype(jnp.bfloat16)


def pack_lines(near, far):
    lane = lax.broadcasted_iota(jnp.int32, near[:, LANES:].shape, 1)
    other = (lane >= 32) & (lane < 96)
    tail = jnp.where(other, pltpu.roll(far[:, :LANES], 64, 1), near[:, :LANES])
    return jnp.concatenate([near[:, LANES:], far[:, LANES:], tail], axis=1)


def roll_tables(raw_ref, pick_ref, first_ref, second_ref, lines):
    heads = raw_ref.shape[0]
    length = raw_ref.shape[2]
    tiles = -(-length // LANES)
    lines[:, 64:96, LANES:] = jnp.zeros((heads, 32, LANES), jnp.float32)
    for tile in range(tiles):
        size = min(LANES, length - tile * LANES)
        block = raw_ref[:, :, tile * LANES : tile * LANES + size].astype(jnp.float32)
        for line in (tile, tile - 1):
            side = (tile - line) * LANES
            if line < 0:
                continue
            if line < 32:
                place = 31 - line
                lines[:, 2 * place : 2 * place + 2, side : side + size] = block
            if line >= 33:
                place = 47 - (line - 33)
                if place >= 32:
                    lines[:, 2 * place : 2 * place + 2, side : side + size] = block
    for head in range(heads):
        rolled = jnp.concatenate(
            [
                pltpu.roll(lines[head, :64], 0, 1, stride=2, stride_axis=0),
                pltpu.roll(lines[head, 64:], 64, 1, stride=2, stride_axis=0),
            ],
            axis=0,
        ).astype(jnp.bfloat16)
        rows = exact(pick_ref[...], rolled)
        first = pltpu.roll(rows[:48], 2, 1)
        at = slice(head * GROUP, (head + 1) * GROUP)
        first_ref[at] = pack_lines(first[:24], first[24:]).astype(jnp.bfloat16)
        second_ref[at] = pack_lines(rows[48:72], rows[72:]).astype(jnp.bfloat16)


def dense_groups(table, lanes, rows, groups):
    spread = exact(table, lanes)
    for group in range(groups):
        part = spread[group * GROUP : (group + 1) * GROUP]
        stacked = jnp.concatenate(
            [part[:, w * PAD : w * PAD + TOKENS] for w in range(WW)], axis=0
        ).astype(jnp.bfloat16)
        yield group, exact(rows, stacked)


def attend(packed, bias, heads):
    rows, width = packed.shape[0], packed.shape[1] // 3
    head_dim = width // heads
    per_tile = LANES // head_dim
    lane = lax.broadcasted_iota(jnp.int32, (rows, LANES), 1) // head_dim
    ones = jnp.ones((rows, LANES), jnp.bfloat16)
    tiles = []
    for start in range(0, width, LANES):
        query, keys, values = (
            packed[:, start + i * width : start + i * width + LANES] for i in range(3)
        )
        values = jnp.concatenate([values, ones], axis=1)
        total = jnp.zeros((rows, LANES), jnp.float32)
        for part in range(per_tile):
            mine = lane == part
            chosen = jnp.where(mine, query, jnp.zeros_like(query))
            scores = lax.dot_general(
                chosen, keys, (((1,), (1,)), ((), ())), preferred_element_type=jnp.float32
            )
            scores = scores * head_dim ** (-0.5) + bias(start // head_dim + part).astype(jnp.float32)
            top = jnp.max(scores, axis=-1, keepdims=True)
            weights = jnp.exp2((scores - top) * LOG2E).astype(jnp.bfloat16)
            mixed = jnp.dot(weights, values, preferred_element_type=jnp.float32)
            total = jnp.where(mine, mixed[:, :LANES] / mixed[:, LANES:], total)
        tiles.append(total)
    return jnp.concatenate(tiles, axis=1)


def inner_columns(rows, width):
    index = lax.broadcasted_iota(jnp.int32, (rows, width), 0)
    return index - jnp.where(index >= CELLS, CELLS, 0) < SIDE


def first_kernel(
    heads, raw_ref, pick_ref, field_ref, gain_ref, offset_ref, qkv_w, qkv_b, proj_w, proj_b,
    lanes_ref, rows_ref, order_ref, back_ref, first_ref, second_ref, bias_ref, table1_ref, core_ref,
    lines, table_ref,
):
    roll_tables(raw_ref, pick_ref, table_ref, table1_ref, lines)
    for head, dense in dense_groups(table_ref[...], lanes_ref[...], rows_ref[...], heads):
        bias_ref[head] = dense.astype(jnp.bfloat16)
    cells, depth, width = field_ref.shape
    grid = field_ref[...].reshape(cells * depth, width)
    tokens = normalized(grid, gain_ref[0:1], offset_ref[0:1])
    tokens = exact(order_ref[...], tokens).astype(jnp.bfloat16)
    packed = jnp.dot(tokens, qkv_w[...], preferred_element_type=jnp.float32) + qkv_b[0:1]
    packed = packed.astype(jnp.bfloat16)
    for window in range(2):
        at = slice(window * TOKENS, (window + 1) * TOKENS)
        core_ref[at] = attend(packed[at], bias_ref.__getitem__, heads)
    core = exact(back_ref[...], core_ref[...].astype(jnp.bfloat16)).astype(jnp.bfloat16)
    result = jnp.dot(core, proj_w[...], preferred_element_type=jnp.float32) + proj_b[0:1]
    first = grid + result
    first_ref[...] = first
    second_ref[...] = normalized(first, gain_ref[1:2], offset_ref[1:2])


def edge_kernel(
    heads, second_ref, near_ref, wrap_ref, gain_ref, offset_ref, qkv_w, qkv_b, proj_w,
    proj_b, bias_ref, side_ref, strip_ref, edge_ref, send_ref, keep_ref, core_ref,
):
    width = second_ref.shape[1]
    near = near_ref[...].astype(jnp.float32).reshape(TOKENS, width)
    wrap = wrap_ref[...].astype(jnp.float32).reshape(TOKENS, width)
    odd = lax.rem(lax.axis_index("lon"), 2) == 1
    left = exact(side_ref[...], jnp.where(odd, near, wrap).astype(jnp.bfloat16))
    right = exact(side_ref[...], jnp.where(odd, wrap, near).astype(jnp.bfloat16))
    tokens = normalized(jnp.concatenate([left, right], axis=0), gain_ref[0:1], offset_ref[0:1])
    packed = jnp.dot(tokens, qkv_w[...], preferred_element_type=jnp.float32) + qkv_b[0:1]
    packed = packed.astype(jnp.bfloat16)
    for window in range(2):
        at = slice(window * TOKENS, (window + 1) * TOKENS)
        core_ref[at] = attend(packed[at], bias_ref.__getitem__, heads)
    inner = inner_columns(TOKENS, width)
    core = jnp.where(inner, core_ref[TOKENS:], core_ref[:TOKENS]).astype(jnp.bfloat16)
    result = jnp.dot(core, proj_w[...], preferred_element_type=jnp.float32) + proj_b[0:1]
    edge = jnp.where(inner, right, left) + result
    edge = normalized(edge, gain_ref[1:2], offset_ref[1:2])
    strip = exact(strip_ref[...], second_ref[...]) + exact(edge_ref[...], edge)
    half = strip.shape[0] // 2
    send_ref[...] = strip[:half].astype(jnp.bfloat16)
    keep_ref[...] = strip[half:].astype(jnp.bfloat16)


def bias_kernel(heads, table_ref, lanes_ref, rows_ref, out_ref):
    upper = lax.broadcasted_iota(jnp.int32, (TOKENS, TOKENS), 0) < CELLS
    left = lax.broadcasted_iota(jnp.int32, (TOKENS, TOKENS), 1) < CELLS
    last = lax.axis_index("lat") == lax.axis_size("lat") - 1
    flag = jnp.where(last, 1.0, 0.0)
    barred = jnp.where(upper != left, flag * -1000000000.0, 0.0)
    for head, dense in dense_groups(table_ref[...], lanes_ref[...], rows_ref[...], heads):
        out_ref[head] = (dense + barred).astype(jnp.bfloat16)


def second_kernel(
    heads, own_ref, got_ref, qkv_w, qkv_b, proj_w, proj_b, bias_ref, back_ref, keep_ref, send_ref,
    core_ref,
):
    width = own_ref.shape[1]
    own, got = own_ref[...].astype(jnp.float32), got_ref[...].astype(jnp.float32)
    tokens = []
    for window in range(3):
        at = slice(window * CELLS, (window + 1) * CELLS)
        tokens += [own[at], got[at]]
    tokens = jnp.concatenate(tokens, axis=0).astype(jnp.bfloat16)
    packed = jnp.dot(tokens, qkv_w[...], preferred_element_type=jnp.float32) + qkv_b[1:2]
    packed = packed.astype(jnp.bfloat16)
    for window in range(3):
        at = slice(window * TOKENS, (window + 1) * TOKENS)
        core_ref[window] = attend(packed[at], bias_ref.__getitem__, heads)
    inner = inner_columns(CELLS, width)
    for start, out_ref in ((CELLS, send_ref), (0, keep_ref)):
        at = slice(start, start + CELLS)
        outer = jnp.where(inner, core_ref[2, at], core_ref[0, at])
        core = jnp.concatenate([core_ref[1, at], outer], axis=0).astype(jnp.bfloat16)
        core = exact(back_ref[...], core).astype(jnp.bfloat16)
        result = jnp.dot(core, proj_w[...], preferred_element_type=jnp.float32) + proj_b[1:2]
        out_ref[...] = result.astype(out_ref.dtype)


def final_kernel(first_ref, keep_ref, got_ref, out_ref):
    got = got_ref[...].astype(jnp.float32)
    result = first_ref[...] + jnp.concatenate([got, keep_ref[...]], axis=0)
    out_ref[...] = result.reshape(out_ref.shape)


def exchanged(block, near):
    count = lax.axis_size("lon")
    partner = [i ^ 1 if near else (i + (1 if i % 2 else -1)) % count for i in range(count)]
    return lax.ppermute(block, "lon", [(i, partner[i]) for i in range(count)])


def passed_along(block, axis, distance):
    count = lax.axis_size(axis)
    return lax.ppermute(block, axis, [((i - distance) % count, i) for i in range(count)])


WHOLE = lambda shape: pl.BlockSpec(shape, lambda i: (0,) * len(shape))


def chosen(array, which):
    size = array.shape[1:]
    return pl.BlockSpec((None, *size), lambda i: (which,) + (0,) * len(size))


def run(kernel, name, operands, specs, outs, scratch=(), limit=VMEM_LIMIT):
    specs = [WHOLE(x.shape) if s is None else s for x, s in zip(operands, specs, strict=True)]
    return pl.pallas_call(
        kernel,
        grid=(1,),
        out_shape=[jax.ShapeDtypeStruct(*out) for out in outs],
        in_specs=specs,
        out_specs=[WHOLE(shape) for shape, _ in outs],
        scratch_shapes=list(scratch),
        compiler_params=pltpu.CompilerParams(vmem_limit_bytes=limit),
        cost_estimate=pl.CostEstimate(flops=10**9, bytes_accessed=4000000, transcendentals=0),
        name=name,
    )(*operands)


def per_device(
    field, norm_gain, norm_bias, qkv_weight, qkv_bias, proj_weight, proj_bias, earth_bias
):
    depth, lat_rows, lon_cols, width = field.shape
    heads = earth_bias.shape[2]
    f32, bf16 = jnp.float32, jnp.bfloat16
    native = jnp.transpose(field, (1, 2, 0, 3))
    raw = jnp.transpose(earth_bias[:, 0], (1, 0, 2))

    halves = native.astype(bf16)
    odd = lax.axis_index("lon") % 2 == 1
    to_wrap = jnp.where(odd, halves[:, WW:], halves[:, :WW])
    to_near = jnp.where(odd, halves[:, :WW], halves[:, WW:])
    wrap = exchanged(to_wrap, False)
    near = exchanged(to_near, True)

    rows = heads * WH
    lanes = const(lane_selector())
    strip = (lon_cols + WW) * Z * HALF
    cells = lat_rows * lon_cols
    first, second, bias0, table1 = run(
        functools.partial(first_kernel, heads),
        "first_block",
        (
            raw, const(table_rows()), native.reshape(cells, depth, width), norm_gain, norm_bias, qkv_weight, qkv_bias,
            proj_weight, proj_bias, lanes, const(full_rows()),
            const(native_to_windows(2)), const(windows_to_native(2)),
        ),
        (None,) * 5 + (chosen(qkv_weight, 0), None, chosen(proj_weight, 0)) + (None,) * 5,
        [
            ((cells * depth, width), f32), ((cells * depth, width), bf16),
            ((heads, TOKENS, TOKENS), bf16), ((2 * rows, PACKED), bf16),
        ],
        [
            pltpu.VMEM((2 * TOKENS, width), f32),
            pltpu.VMEM((heads, 96, PAD), f32),
            pltpu.VMEM((2 * rows, PACKED), bf16),
        ],
    )
    send, keep = run(
        functools.partial(edge_kernel, heads),
        "first_block_edges",
        (
            second, near.reshape(cells // 2, depth, width),
            wrap.reshape(cells // 2, depth, width), norm_gain, norm_bias, qkv_weight, qkv_bias,
            proj_weight, proj_bias, bias0, const(native_to_windows(1)),
            const(strip_from_native(lon_cols)), const(strip_from_sides(lon_cols)),
        ),
        (None, None, None, None, None, chosen(qkv_weight, 0), None, chosen(proj_weight, 0))
        + (None,) * 5,
        [((strip, width), bf16), ((strip, width), bf16)],
        [pltpu.VMEM((2 * TOKENS, width), f32)],
        limit=VMEM_SHARED,
    )
    from_above = passed_along(send, "lat", -1)
    (bias1,) = run(
        functools.partial(bias_kernel, heads),
        "second_bias",
        (table1, lanes, const(full_rows())),
        (None, None, None),
        [((heads, TOKENS, TOKENS), bf16)],
        limit=VMEM_SHARED,
    )
    kept, leaving = run(
        functools.partial(second_kernel, heads),
        "second_block",
        (
            keep, from_above, qkv_weight, qkv_bias, proj_weight, proj_bias, bias1,
            const(native_from_queries()),
        ),
        (None, None, chosen(qkv_weight, 1), None, chosen(proj_weight, 1)) + (None,) * 3,
        [((TOKENS, width), f32), ((TOKENS, width), bf16)],
        [pltpu.VMEM((3, TOKENS, width), f32)],
        limit=VMEM_SHARED,
    )
    from_below = passed_along(leaving, "lat", 1)
    (mixed,) = run(
        final_kernel,
        "final_sum",
        (first, kept, from_below),
        (None,) * 3,
        [((cells, depth, width), f32)],
        limit=VMEM_SHARED,
    )
    return jnp.transpose(mixed.reshape(lat_rows, lon_cols, depth, width), (2, 0, 1, 3))


def solution(mesh):
    in_specs = (P(None, "lat", "lon", None), P(), P(), P(), P(), P(), P(), P(None, "lat", None, None))
    out_specs = P(None, "lat", "lon", None)
    return jax.shard_map(
        per_device, mesh=mesh, in_specs=in_specs, out_specs=out_specs, check_vma=False
    )
```

```python
import functools

import jax
import jax.numpy as jnp
import numpy as np
from jax import lax
from jax.experimental import pallas as pl
from jax.experimental.pallas import tpu as pltpu
from jax.sharding import PartitionSpec as P

Z = 2
WH = 12
WW = 6
HALF = WH // 2
SPAN = 2 * WW - 1
CELLS = WW * Z * HALF
TOKENS = 2 * CELLS
SIDE = CELLS // 2
GROUP = Z * WH
LANES = 128
PAD = 256
PACKED = 3 * LANES
LINE = WH * SPAN
LOG2E = float(np.log2(np.e))
VMEM_LIMIT = 60 * 1024 * 1024
VMEM_SHARED = 40 * 1024 * 1024


def grid_of(*sizes):
    return [part.reshape(-1) for part in np.meshgrid(*map(np.arange, sizes), indexing="ij")]


def one_hot(rows, columns, width):
    table = np.zeros((len(rows), width), np.float32)
    keep = columns >= 0
    table[np.arange(len(rows))[keep], columns[keep]] = 1.0
    return table


def packed_lane(level, entry):
    lane = (entry + LANES - 2) % PAD
    tail = 2 * LANES + (lane + 64 * level) % LANES
    return np.where(lane >= LANES, level * LANES + lane - LANES, tail)


def lane_selector():
    half, col, level, row = grid_of(2, WW, Z, HALF)
    row = row + half * HALF
    table = np.zeros((PACKED, WW, PAD), np.float32)
    for w in range(WW):
        entry = row * SPAN + w - col + WW - 1
        table[packed_lane(level, entry), w, np.arange(TOKENS)] = 1.0
    return table.reshape(PACKED, WW * PAD)


def full_rows():
    half, col, level, row = grid_of(2, WW, Z, HALF)
    place = col * GROUP + level * WH + half * HALF + row
    return one_hot(place, place, TOKENS)


def table_rows():
    position = np.concatenate([31 - np.arange(32), 47 - np.arange(16)])
    picks = []
    for block in range(2):
        for key_level in range(Z):
            level, row = grid_of(Z, WH)
            picks.append(2 * position[(level * Z + key_level) * WH + row] + block)
    picks = np.concatenate(picks)
    return one_hot(picks, picks, 96)


def native_to_windows(windows):
    window, half, col, level, row = grid_of(windows, 2, WW, Z, HALF)
    place = ((half * HALF + row) * windows * WW + window * WW + col) * Z + level
    return one_hot(place, place, len(place))


def windows_to_native(windows):
    return native_to_windows(windows).T


def strip_from_native(cols):
    half, col, level, row = grid_of(2, cols + WW, Z, HALF)
    own = col - WW // 2
    place = ((half * HALF + row) * cols + own) * Z + level
    place = np.where((own >= 0) & (own < cols), place, -1)
    return one_hot(place, place, WH * cols * Z)


def strip_from_sides(cols):
    half, col, level, row = grid_of(2, cols + WW, Z, HALF)
    own = col - WW // 2
    inside = np.where(own < 0, own + WW, own - cols)
    place = ((half * WW + inside) * Z + level) * HALF + row
    place = np.where((own >= 0) & (own < cols), -1, place)
    return one_hot(place, place, TOKENS)


def native_from_queries():
    row, col, level = grid_of(HALF, 2 * WW, Z)
    middle = (col >= 3) & (col < 9)
    column = np.where(middle, col - 3, np.where(col < 3, col + 3, col - 9))
    place = ((np.where(middle, 0, 1) * WW + column) * Z + level) * HALF + row
    return one_hot(place, place, TOKENS)


def const(table):
    return jnp.asarray(table, jnp.bfloat16)


def exact(table, rows):
    return jnp.dot(table, rows, preferred_element_type=jnp.float32)


def normalized(grid, gain, offset):
    center = grid - jnp.mean(grid, axis=-1, keepdims=True)
    spread = jnp.mean(center * center, axis=-1, keepdims=True)
    return (center * lax.rsqrt(spread + 1e-05) * gain + offset).astype(jnp.bfloat16)


def pack_lines(near, far):
    lane = lax.broadcasted_iota(jnp.int32, near[:, LANES:].shape, 1)
    other = (lane >= 32) & (lane < 96)
    tail = jnp.where(other, pltpu.roll(far[:, :LANES], 64, 1), near[:, :LANES])
    return jnp.concatenate([near[:, LANES:], far[:, LANES:], tail], axis=1)


def roll_tables(raw_ref, pick_ref, first_ref, second_ref, lines):
    heads = raw_ref.shape[0]
    length = raw_ref.shape[2]
    tiles = -(-length // LANES)
    lines[:, 64:96, LANES:] = jnp.zeros((heads, 32, LANES), jnp.float32)
    for tile in range(tiles):
        size = min(LANES, length - tile * LANES)
        block = raw_ref[:, :, tile * LANES : tile * LANES + size].astype(jnp.float32)
        for line in (tile, tile - 1):
            side = (tile - line) * LANES
            if line < 0:
                continue
            if line < 32:
                place = 31 - line
                lines[:, 2 * place : 2 * place + 2, side : side + size] = block
            if line >= 33:
                place = 47 - (line - 33)
                if place >= 32:
                    lines[:, 2 * place : 2 * place + 2, side : side + size] = block
    for head in range(heads):
        rolled = jnp.concatenate(
            [
                pltpu.roll(lines[head, :64], 0, 1, stride=2, stride_axis=0),
                pltpu.roll(lines[head, 64:], 64, 1, stride=2, stride_axis=0),
            ],
            axis=0,
        ).astype(jnp.bfloat16)
        rows = exact(pick_ref[...], rolled)
        first = pltpu.roll(rows[:48], 2, 1)
        at = slice(head * GROUP, (head + 1) * GROUP)
        first_ref[at] = pack_lines(first[:24], first[24:]).astype(jnp.bfloat16)
        second_ref[at] = pack_lines(rows[48:72], rows[72:]).astype(jnp.bfloat16)


def dense_groups(table, lanes, rows, groups):
    spread = exact(table, lanes)
    for group in range(groups):
        part = spread[group * GROUP : (group + 1) * GROUP]
        stacked = jnp.concatenate(
            [part[:, w * PAD : w * PAD + TOKENS] for w in range(WW)], axis=0
        ).astype(jnp.bfloat16)
        yield group, exact(rows, stacked)


def attend(packed, bias, heads):
    rows, width = packed.shape[0], packed.shape[1] // 3
    head_dim = width // heads
    per_tile = LANES // head_dim
    lane = lax.broadcasted_iota(jnp.int32, (rows, LANES), 1) // head_dim
    ones = jnp.ones((rows, LANES), jnp.bfloat16)
    tiles = []
    for start in range(0, width, LANES):
        query, keys, values = (
            packed[:, start + i * width : start + i * width + LANES] for i in range(3)
        )
        values = jnp.concatenate([values, ones], axis=1)
        total = jnp.zeros((rows, LANES), jnp.float32)
        for part in range(per_tile):
            mine = lane == part
            chosen = jnp.where(mine, query, jnp.zeros_like(query))
            scores = lax.dot_general(
                chosen, keys, (((1,), (1,)), ((), ())), preferred_element_type=jnp.float32
            )
            scores = scores * head_dim ** (-0.5) + bias(start // head_dim + part).astype(jnp.float32)
            top = jnp.max(scores, axis=-1, keepdims=True)
            weights = jnp.exp2((scores - top) * LOG2E).astype(jnp.bfloat16)
            mixed = jnp.dot(weights, values, preferred_element_type=jnp.float32)
            total = jnp.where(mine, mixed[:, :LANES] / mixed[:, LANES:], total)
        tiles.append(total)
    return jnp.concatenate(tiles, axis=1)


def inner_columns(rows, width):
    index = lax.broadcasted_iota(jnp.int32, (rows, width), 0)
    return index - jnp.where(index >= CELLS, CELLS, 0) < SIDE


def first_kernel(
    heads, raw_ref, pick_ref, field_ref, gain_ref, offset_ref, qkv_w, qkv_b, proj_w, proj_b,
    lanes_ref, rows_ref, order_ref, back_ref, first_ref, second_ref, bias_ref, table1_ref, core_ref,
    lines, table_ref,
):
    roll_tables(raw_ref, pick_ref, table_ref, table1_ref, lines)
    for head, dense in dense_groups(table_ref[...], lanes_ref[...], rows_ref[...], heads):
        bias_ref[head] = dense.astype(jnp.bfloat16)
    cells, depth, width = field_ref.shape
    grid = field_ref[...].reshape(cells * depth, width)
    tokens = normalized(grid, gain_ref[0:1], offset_ref[0:1])
    tokens = exact(order_ref[...], tokens).astype(jnp.bfloat16)
    packed = jnp.dot(tokens, qkv_w[...], preferred_element_type=jnp.float32) + qkv_b[0:1]
    packed = packed.astype(jnp.bfloat16)
    for window in range(2):
        at = slice(window * TOKENS, (window + 1) * TOKENS)
        core_ref[at] = attend(packed[at], bias_ref.__getitem__, heads)
    core = exact(back_ref[...], core_ref[...].astype(jnp.bfloat16)).astype(jnp.bfloat16)
    result = jnp.dot(core, proj_w[...], preferred_element_type=jnp.float32) + proj_b[0:1]
    first = grid + result
    first_ref[...] = first
    second_ref[...] = normalized(first, gain_ref[1:2], offset_ref[1:2])


def edge_kernel(
    heads, second_ref, near_ref, wrap_ref, gain_ref, offset_ref, qkv_w, qkv_b, proj_w,
    proj_b, bias_ref, side_ref, strip_ref, edge_ref, send_ref, keep_ref, core_ref,
    bias_here, second_here, bias_sem, second_sem,
):
    bias_copy = pltpu.make_async_copy(bias_ref, bias_here, bias_sem)
    second_copy = pltpu.make_async_copy(second_ref, second_here, second_sem)
    bias_copy.start()
    second_copy.start()
    width = second_ref.shape[1]
    near = near_ref[...].astype(jnp.float32).reshape(TOKENS, width)
    wrap = wrap_ref[...].astype(jnp.float32).reshape(TOKENS, width)
    odd = lax.rem(lax.axis_index("lon"), 2) == 1
    left = exact(side_ref[...], jnp.where(odd, near, wrap).astype(jnp.bfloat16))
    right = exact(side_ref[...], jnp.where(odd, wrap, near).astype(jnp.bfloat16))
    tokens = normalized(jnp.concatenate([left, right], axis=0), gain_ref[0:1], offset_ref[0:1])
    packed = jnp.dot(tokens, qkv_w[...], preferred_element_type=jnp.float32) + qkv_b[0:1]
    packed = packed.astype(jnp.bfloat16)
    bias_copy.wait()
    for window in range(2):
        at = slice(window * TOKENS, (window + 1) * TOKENS)
        core_ref[at] = attend(packed[at], bias_here.__getitem__, heads)
    inner = inner_columns(TOKENS, width)
    core = jnp.where(inner, core_ref[TOKENS:], core_ref[:TOKENS]).astype(jnp.bfloat16)
    result = jnp.dot(core, proj_w[...], preferred_element_type=jnp.float32) + proj_b[0:1]
    edge = jnp.where(inner, right, left) + result
    edge = normalized(edge, gain_ref[1:2], offset_ref[1:2])
    second_copy.wait()
    strip = exact(strip_ref[...], second_here[...]) + exact(edge_ref[...], edge)
    half = strip.shape[0] // 2
    send_ref[...] = strip[:half].astype(jnp.bfloat16)
    keep_ref[...] = strip[half:].astype(jnp.bfloat16)


def bias_kernel(heads, table_ref, lanes_ref, rows_ref, out_ref):
    upper = lax.broadcasted_iota(jnp.int32, (TOKENS, TOKENS), 0) < CELLS
    left = lax.broadcasted_iota(jnp.int32, (TOKENS, TOKENS), 1) < CELLS
    last = lax.axis_index("lat") == lax.axis_size("lat") - 1
    flag = jnp.where(last, 1.0, 0.0)
    barred = jnp.where(upper != left, flag * -1000000000.0, 0.0)
    for head, dense in dense_groups(table_ref[...], lanes_ref[...], rows_ref[...], heads):
        out_ref[head] = (dense + barred).astype(jnp.bfloat16)


def second_kernel(
    heads, own_ref, got_ref, qkv_w, qkv_b, proj_w, proj_b, bias_ref, back_ref, keep_ref, send_ref,
    core_ref,
):
    width = own_ref.shape[1]
    own, got = own_ref[...].astype(jnp.float32), got_ref[...].astype(jnp.float32)
    tokens = []
    for window in range(3):
        at = slice(window * CELLS, (window + 1) * CELLS)
        tokens += [own[at], got[at]]
    tokens = jnp.concatenate(tokens, axis=0).astype(jnp.bfloat16)
    packed = jnp.dot(tokens, qkv_w[...], preferred_element_type=jnp.float32) + qkv_b[1:2]
    packed = packed.astype(jnp.bfloat16)
    for window in range(3):
        at = slice(window * TOKENS, (window + 1) * TOKENS)
        core_ref[window] = attend(packed[at], bias_ref.__getitem__, heads)
    inner = inner_columns(CELLS, width)
    for start, out_ref in ((CELLS, send_ref), (0, keep_ref)):
        at = slice(start, start + CELLS)
        outer = jnp.where(inner, core_ref[2, at], core_ref[0, at])
        core = jnp.concatenate([core_ref[1, at], outer], axis=0).astype(jnp.bfloat16)
        core = exact(back_ref[...], core).astype(jnp.bfloat16)
        result = jnp.dot(core, proj_w[...], preferred_element_type=jnp.float32) + proj_b[1:2]
        out_ref[...] = result.astype(out_ref.dtype)


def final_kernel(first_ref, keep_ref, got_ref, out_ref):
    got = got_ref[...].astype(jnp.float32)
    result = first_ref[...] + jnp.concatenate([got, keep_ref[...]], axis=0)
    out_ref[...] = result.reshape(out_ref.shape)


def exchanged(block, near):
    count = lax.axis_size("lon")
    partner = [i ^ 1 if near else (i + (1 if i % 2 else -1)) % count for i in range(count)]
    return lax.ppermute(block, "lon", [(i, partner[i]) for i in range(count)])


def passed_along(block, axis, distance):
    count = lax.axis_size(axis)
    return lax.ppermute(block, axis, [((i - distance) % count, i) for i in range(count)])


ANY = pl.BlockSpec(memory_space=pl.ANY)
WHOLE = lambda shape: pl.BlockSpec(shape, lambda i: (0,) * len(shape))


def chosen(array, which):
    size = array.shape[1:]
    return pl.BlockSpec((None, *size), lambda i: (which,) + (0,) * len(size))


def run(kernel, name, operands, specs, outs, scratch=(), limit=VMEM_LIMIT):
    specs = [WHOLE(x.shape) if s is None else s for x, s in zip(operands, specs, strict=True)]
    return pl.pallas_call(
        kernel,
        grid=(1,),
        out_shape=[jax.ShapeDtypeStruct(*out) for out in outs],
        in_specs=specs,
        out_specs=[WHOLE(shape) for shape, _ in outs],
        scratch_shapes=list(scratch),
        compiler_params=pltpu.CompilerParams(vmem_limit_bytes=limit),
        cost_estimate=pl.CostEstimate(flops=10**9, bytes_accessed=4000000, transcendentals=0),
        name=name,
    )(*operands)


def per_device(
    field, norm_gain, norm_bias, qkv_weight, qkv_bias, proj_weight, proj_bias, earth_bias
):
    depth, lat_rows, lon_cols, width = field.shape
    heads = earth_bias.shape[2]
    f32, bf16 = jnp.float32, jnp.bfloat16
    native = jnp.transpose(field, (1, 2, 0, 3))
    raw = jnp.transpose(earth_bias[:, 0], (1, 0, 2))

    halves = native.astype(bf16)
    odd = lax.axis_index("lon") % 2 == 1
    to_wrap = jnp.where(odd, halves[:, WW:], halves[:, :WW])
    to_near = jnp.where(odd, halves[:, :WW], halves[:, WW:])
    wrap = exchanged(to_wrap, False)
    near = exchanged(to_near, True)

    rows = heads * WH
    lanes = const(lane_selector())
    strip = (lon_cols + WW) * Z * HALF
    cells = lat_rows * lon_cols
    first, second, bias0, table1 = run(
        functools.partial(first_kernel, heads),
        "first_block",
        (
            raw, const(table_rows()), native.reshape(cells, depth, width), norm_gain, norm_bias, qkv_weight, qkv_bias,
            proj_weight, proj_bias, lanes, const(full_rows()),
            const(native_to_windows(2)), const(windows_to_native(2)),
        ),
        (None,) * 5 + (chosen(qkv_weight, 0), None, chosen(proj_weight, 0)) + (None,) * 5,
        [
            ((cells * depth, width), f32), ((cells * depth, width), bf16),
            ((heads, TOKENS, TOKENS), bf16), ((2 * rows, PACKED), bf16),
        ],
        [
            pltpu.VMEM((2 * TOKENS, width), f32),
            pltpu.VMEM((heads, 96, PAD), f32),
            pltpu.VMEM((2 * rows, PACKED), bf16),
        ],
    )
    send, keep = run(
        functools.partial(edge_kernel, heads),
        "first_block_edges",
        (
            second, near.reshape(cells // 2, depth, width),
            wrap.reshape(cells // 2, depth, width), norm_gain, norm_bias, qkv_weight, qkv_bias,
            proj_weight, proj_bias, bias0, const(native_to_windows(1)),
            const(strip_from_native(lon_cols)), const(strip_from_sides(lon_cols)),
        ),
        (ANY, None, None, None, None, chosen(qkv_weight, 0), None, chosen(proj_weight, 0), None, ANY)
        + (None,) * 3,
        [((strip, width), bf16), ((strip, width), bf16)],
        [
            pltpu.VMEM((2 * TOKENS, width), f32),
            pltpu.VMEM((heads, TOKENS, TOKENS), bf16),
            pltpu.VMEM((cells * depth, width), bf16),
            pltpu.SemaphoreType.DMA,
            pltpu.SemaphoreType.DMA,
        ],
        limit=VMEM_SHARED,
    )
    from_above = passed_along(send, "lat", -1)
    (bias1,) = run(
        functools.partial(bias_kernel, heads),
        "second_bias",
        (table1, lanes, const(full_rows())),
        (None, None, None),
        [((heads, TOKENS, TOKENS), bf16)],
        limit=VMEM_SHARED,
    )
    kept, leaving = run(
        functools.partial(second_kernel, heads),
        "second_block",
        (
            keep, from_above, qkv_weight, qkv_bias, proj_weight, proj_bias, bias1,
            const(native_from_queries()),
        ),
        (None, None, chosen(qkv_weight, 1), None, chosen(proj_weight, 1)) + (None,) * 3,
        [((TOKENS, width), f32), ((TOKENS, width), bf16)],
        [pltpu.VMEM((3, TOKENS, width), f32)],
        limit=VMEM_SHARED,
    )
    from_below = passed_along(leaving, "lat", 1)
    (mixed,) = run(
        final_kernel,
        "final_sum",
        (first, kept, from_below),
        (None,) * 3,
        [((cells, depth, width), f32)],
        limit=VMEM_SHARED,
    )
    return jnp.transpose(mixed.reshape(lat_rows, lon_cols, depth, width), (2, 0, 1, 3))


def solution(mesh):
    in_specs = (P(None, "lat", "lon", None), P(), P(), P(), P(), P(), P(), P(None, "lat", None, None))
    out_specs = P(None, "lat", "lon", None)
    return jax.shard_map(
        per_device, mesh=mesh, in_specs=in_specs, out_specs=out_specs, check_vma=False
    )
```
